256 devices in a mesh: row: 16 (over y, z_hi, core), col: 16 (over z_lo, x).
Axes of the slice: x: 4, y: 4, z: 8 (z_hi: 2, z_lo: 4; z = z_hi * 4 + z_lo), core: 2. Of those that a mesh axis runs over, the one named last changes fastest.
Arguments:
- amplitudes: float32 [16, 16, 768, 768], P('row', 'col'), may hold values from -0.6 to 0.6
- integrals: float32 [16, 16, 768, 768], P('row', 'col'), may hold values from -6 to 6
- factors: float32 [16, 2048, 768], P('col', 'row'), may hold values from -0.21 to 0.21
- occ_energy: float32 [16], replicated, may hold values from -2 to -0.5
- vir_energy: float32 [768], replicated, may hold values from 0.5 to 3
Outputs:
- new_amplitudes: float32 [16, 16, 768, 768], P('row', 'col')
The draws below stay inside these ranges and needn't reach their ends.
All inputs are finite; a program needn't handle non-finite values.
Results may differ from the reference program's by a relative error of at most 0.00005.
Values sent between devices are 32-bit elements; how exact they have to be, the bound alone decides.
No kernel may reach another device: no remote copies, remote signals or barrier semaphores. Data moves between devices by JAX's collectives and lax.ppermute only.
A program may use at most 128 MiB of HBM per device.

```python
import jax
import jax.numpy as jnp
from jax import lax

O = 16
V = 768
NAUX = 2048


def steps_of(stream_key, extent, shards, smallest, largest):
    gain = 1.0
    for axis_at, parts in shards:
        draws = jax.random.uniform(jax.random.fold_in(jax.random.fold_in(stream_key, 6), axis_at), (parts,), jnp.float32, smallest / len(shards), largest / len(shards))
        gain = gain * jnp.repeat(jnp.exp(draws), extent[axis_at] // parts).reshape((-1,) + (1,) * (len(extent) - 1 - axis_at))
    return gain


def centred(key, shape, width, limit, shards=(), kind=jnp.bfloat16):
    factor_of = steps_of(key, shape, shards, -0.22, 0.18) if shards else 1.0
    array = jax.random.normal(key, shape, jnp.float32) * width * factor_of
    return jnp.minimum(jnp.maximum(array, -limit), limit).astype(kind)


def setup_inputs(seed: int = 0) -> dict:
    key_list = jax.random.split(jax.random.key(seed), 6)
    amplitudes = centred(key_list[0], (O, O, V, V), 0.1, 0.6, ((0, 16), (1, 16)), jnp.float32)
    integrals = centred(key_list[1], (O, O, V, V), 1.0, 6.0, ((0, 16), (1, 16)), jnp.float32)
    factors = centred(key_list[2], (O, NAUX, V), 0.03, 0.21, ((0, 16), (1, 16)), jnp.float32)
    occ_energy = jnp.clip(jax.random.uniform(key_list[3], (O,), jnp.float32, -2.0, -0.5), -2.0, -0.5)
    vir_energy = jnp.clip(jax.random.uniform(key_list[4], (V,), jnp.float32, 0.5, 3.0), 0.5, 3.0)
    return {"amplitudes": amplitudes, "integrals": integrals, "factors": factors, "occ_energy": occ_energy, "vir_energy": vir_energy}


def reference(amplitudes, integrals, factors, occ_energy, vir_energy):
    exact = lax.Precision.HIGHEST

    def one_row(occ_index):
        row_tiles = amplitudes[occ_index]
        col_tiles = jnp.swapaxes(amplitudes[:, occ_index], 1, 2)
        combined = 2.0 * row_tiles - col_tiles
        return jnp.einsum("jab,jpb->pa", combined, factors, precision=exact)

    summed = lax.map(one_row, jnp.arange(O, dtype=jnp.int32))

    def out_row(occ_index):
        direct = jnp.einsum("pa,jpb->jab", summed[occ_index], factors, precision=exact)
        mirror = jnp.einsum("pa,jpb->jab", factors[occ_index], summed, precision=exact)
        denominator = (occ_energy[occ_index] + occ_energy[:, None, None]
                       - vir_energy[None, :, None] - vir_energy[None, None, :])
        return (integrals[occ_index] + direct + mirror) / denominator

    return lax.map(out_row, jnp.arange(O, dtype=jnp.int32))
```

```python
import jax
import jax.numpy as jnp
import numpy as np
from jax import lax
from jax.sharding import Mesh
from jax.sharding import PartitionSpec as P

AXES = ("y", "h", "k", "l", "x1", "x0")
SIZES = (4, 2, 2, 4, 2, 2)
ROW = ("y", "h", "k")
COL = ("l", "x1", "x0")


def send(value, to):
    pairs = []
    for source in range(256):
        y, h, k, l, x1, x0 = (int(v) for v in np.unravel_index(source, SIZES))
        y, h, k, l, x = to(y, h, k, l, 2 * x1 + x0)
        target = np.ravel_multi_index((y % 4, h % 2, k % 2, l % 4, (x % 4) >> 1, x % 2), SIZES)
        pairs.append((source, int(target)))
    return lax.ppermute(value, AXES, pairs)


def to_y(d):
    return lambda y, h, k, l, x: (y + d, h, k, l, x)


def to_x(d):
    return lambda y, h, k, l, x: (y, h, k, l, x + d)


def to_l(d):
    return lambda y, h, k, l, x: (y, h, k, l + d, x)


def to_z(d):
    return lambda y, h, k, l, x: (y, (4 * h + l + d) // 4, k, (l + d) % 4, x)


def to_h(y, h, k, l, x):
    return (y, h + 1, k, l, x)


def to_core(y, h, k, l, x):
    return (y, h, k + 1, l, x)


def to_mirror(y, h, k, l, x):
    return (l, x >> 1, x & 1, y, 2 * h + k)


def spread(d, e):
    return lambda y, h, k, l, x: (y + d, h, x & 1, l, 2 * ((x >> 1) ^ e) + k)


def collect(d, e):
    return lambda y, h, k, l, x: (y + d, h, k, l, x ^ (2 * e))


def pick(value, at):
    return lax.dynamic_index_in_dim(value, at, 0, keepdims=False)


def put(value, block, at):
    return lax.dynamic_update_index_in_dim(value, block, at, 0)


def swap_tile(tile):
    y, h, l, x1 = (lax.axis_index(n) for n in ("y", "h", "l", "x1"))
    z = 4 * h + l
    rows, columns = tile.shape
    parts = tile.reshape(8, rows // 8, columns)
    first = jnp.stack([
        send(pick(parts, 2 * ((y + d) % 4) + (x1 ^ e)), spread(d, e)) for e in range(2) for d in range(4)
    ])
    second = []
    for d in range(8):
        goal = (z + d) % 8
        piece = pick(first, 4 * ((goal >> 2) ^ x1) + (y - (goal & 3)) % 4)
        second.append(send(piece, to_z(d)) if d else piece)
    second = jnp.stack(second)
    out = jnp.zeros_like(parts)
    for e in range(2):
        for d in range(4):
            piece = pick(second, (z - (4 * (x1 ^ e) + (y + d) % 4)) % 8)
            if d or e:
                piece = send(piece, collect(d, e))
            out = put(out, piece, 2 * ((y - d) % 4) + (x1 ^ e))
    return out.reshape(rows, columns)


def reduce_rows(partial):
    y, h, k = (lax.axis_index(n) for n in ROW)
    n, columns = partial.shape
    b = n // 16
    q = partial.reshape(2, 8 * b, columns)
    q = pick(q, k) + send(pick(q, 1 - k), to_core)
    q = q.reshape(4, 2, b, columns)
    far = pick(q, (y + 2) % 4)
    up, down = send(far[0], to_y(1)), send(far[1], to_y(-1))
    after, before = pick(q, (y + 1) % 4), pick(q, (y + 3) % 4)
    after = jnp.stack([after[0] + up, after[1]])
    before = jnp.stack([before[0], before[1] + down])
    r = pick(q, y) + send(after, to_y(1)) + send(before, to_y(-1))
    return pick(r, h) + send(pick(r, 1 - h), to_h)


def gather_rows(block):
    y, h, k = (lax.axis_index(n) for n in ROW)
    b, columns = block.shape
    other = send(block, to_h)
    r = jnp.where(h == 0, jnp.stack([block, other]), jnp.stack([other, block]))
    f, g = send(r, to_y(1)), send(r, to_y(-1))
    e = jnp.stack([send(f[0], to_y(1)), send(g[1], to_y(-1))])
    q = jnp.zeros((4, 2, b, columns), block.dtype)
    for part, at in ((r, y), (f, (y + 3) % 4), (g, (y + 1) % 4), (e, (y + 2) % 4)):
        q = put(q, part, at)
    q = q.reshape(8 * b, columns)
    s = jnp.zeros((2, 8 * b, columns), block.dtype)
    s = put(put(s, q, k), send(q, to_core), 1 - k)
    return s.reshape(16 * b, columns)


def gather_cols(block):
    l, x1, x0 = (lax.axis_index(n) for n in COL)
    x = 2 * x1 + x0
    b, columns = block.shape
    s = jnp.zeros((16, b, columns), block.dtype)
    for d in range(4):
        own = send(block, to_l(d)) if d else block
        f, g = send(own, to_x(1)), send(own, to_x(-1))
        e = jnp.concatenate([send(f[: b // 2], to_x(1)), send(g[b // 2 :], to_x(-1))])
        for part, dx in ((own, 0), (f, 3), (g, 1), (e, 2)):
            from_x = (x + dx) % 4
            s = put(s, part, 8 * (from_x & 1) + 2 * ((l - d) % 4) + (from_x >> 1))
    return s.reshape(16 * b, columns)


def shards(amplitudes, integrals, factors, occ_energy, vir_energy):
    high = lax.Precision.HIGH
    tile, given, block = amplitudes[0, 0], integrals[0, 0], factors[0]
    row = 4 * lax.axis_index("y") + 2 * lax.axis_index("h") + lax.axis_index("k")
    col = 4 * lax.axis_index("l") + 2 * lax.axis_index("x1") + lax.axis_index("x0")

    row_factors = gather_cols(send(block, to_mirror))
    swapped = swap_tile(tile)
    col_factors = gather_rows(block)
    combined = 2.0 * swapped - tile.T
    partial = lax.dot_general(row_factors, combined, (((1,), (1,)), ((), ())), precision=high)
    summed = reduce_rows(partial)
    row_summed = gather_cols(send(summed, to_mirror))
    col_summed = gather_rows(summed)
    over_p = (((0,), (0,)), ((), ()))
    coupled = lax.dot_general(row_summed, col_factors, over_p, precision=high)
    mirrored = lax.dot_general(row_factors, col_summed, over_p, precision=high)
    denominator = occ_energy[row] + occ_energy[col] - vir_energy[:, None] - vir_energy[None, :]
    return ((given + coupled + mirrored) / denominator)[None, None]


def solution(mesh):
    fine = Mesh(mesh.devices.reshape(SIZES), AXES)
    return jax.shard_map(
        shards,
        mesh=fine,
        in_specs=(P(ROW, COL), P(ROW, COL), P(COL, ROW), P(), P()),
        out_specs=P(ROW, COL),
        check_vma=False,
    )
```

```python
import jax
import jax.numpy as jnp
import numpy as np
from jax import lax
from jax.sharding import Mesh
from jax.sharding import PartitionSpec as P

AXES = ("y", "h", "k", "l", "x1", "x0")
SIZES = (4, 2, 2, 4, 2, 2)
ROW = ("y", "h", "k")
COL = ("l", "x1", "x0")


def send(value, to):
    pairs = []
    for source in range(256):
        y, h, k, l, x1, x0 = (int(v) for v in np.unravel_index(source, SIZES))
        y, h, k, l, x = to(y, h, k, l, 2 * x1 + x0)
        target = np.ravel_multi_index((y % 4, h % 2, k % 2, l % 4, (x % 4) >> 1, x % 2), SIZES)
        pairs.append((source, int(target)))
    return lax.ppermute(value, AXES, pairs)


def to_y(d):
    return lambda y, h, k, l, x: (y + d, h, k, l, x)


def to_h(y, h, k, l, x):
    return (y, h + 1, k, l, x)


def to_core(y, h, k, l, x):
    return (y, h, k + 1, l, x)


def pick(value, at):
    return lax.dynamic_index_in_dim(value, at, 0, keepdims=False)


def put(value, block, at):
    return lax.dynamic_update_index_in_dim(value, block, at, 0)


def place(y, h, k):
    return 8 * k + 4 * (y >> 1) + 2 * h + (y & 1)


def to_own_row(y, h, k, l, x):
    col = place(y, h, k)
    return (l, x >> 1, x & 1, col >> 2, col & 3)


def to_own_col(y, h, k, l, x):
    return (2 * (l & 1) + (x & 1), x >> 1, l >> 1, y, 2 * h + k)


def together(*values):
    return lax.optimization_barrier(values)


def get_y(q, y):
    _, n, _, b, columns = q.shape
    return lax.dynamic_slice(q, (y >> 1, 0, y & 1, 0, 0), (1, n, 1, b, columns)).reshape(n, b, columns)


def put_y(q, pair, y):
    n, b, columns = pair.shape
    return lax.dynamic_update_slice(q, pair.reshape(1, n, 1, b, columns), (y >> 1, 0, y & 1, 0, 0))


def shards(amplitudes, integrals, factors, occ_energy, vir_energy):
    high = lax.Precision.HIGH
    tile, given, block = amplitudes[0, 0], integrals[0, 0], factors[0]
    y, h, k, l, x1, x0 = (lax.axis_index(n) for n in AXES)
    row, col = 4 * y + 2 * h + k, 4 * l + 2 * x1 + x0
    b, columns = block.shape

    empty_half = jnp.zeros((2, 2, 2, b, columns), block.dtype)
    empty = jnp.zeros((2, 8 * b, columns), block.dtype)

    def gather_rows(block):
        other = send(block, to_h)
        pair = jnp.where(h == 0, jnp.stack([block, other]), jnp.stack([other, block]))
        f, g = together(send(pair, to_y(1)), send(pair, to_y(-1)))
        e = together(send(f[0], to_y(1)), send(g[1], to_y(-1)))
        q = empty_half
        for part, dy in ((pair, 0), (f, 3), (g, 1), (jnp.stack(e), 2)):
            q = put_y(q, part, (y + dy) % 4)
        q = q.reshape(8 * b, columns)
        return put(put(empty, q, k), send(q, to_core), 1 - k).reshape(16 * b, columns)

    moved, tile, block = together(send(block, to_own_row), tile, block)
    row_factors = lax.all_gather(moved, COL, axis=0, tiled=True)
    col_factors = gather_rows(block)

    direct = lax.dot_general(col_factors, 2.0 * tile, (((1,), (1,)), ((), ())), precision=high)
    direct = lax.psum_scatter(direct, COL, scatter_dimension=0, tiled=True)
    halves = row_factors.reshape(2, 8 * b, columns)
    over_a = (((1,), (0,)), ((), ()))
    theirs = lax.dot_general(pick(halves, 1 - k), tile, over_a, precision=high)
    theirs = send(theirs, to_core)
    q = lax.dot_general(pick(halves, k), tile, over_a, precision=high) + theirs
    q = q.reshape(2, 2, 2, b, columns)
    far = get_y(q, (y + 2) % 4)
    up, down = together(send(far[0], to_y(1)), send(far[1], to_y(-1)))
    after, before = get_y(q, (y + 1) % 4), get_y(q, (y + 3) % 4)
    after = jnp.stack([after[0] + up, after[1]])
    before = jnp.stack([before[0], before[1] + down])
    up, down = together(send(after, to_y(1)), send(before, to_y(-1)))
    r = get_y(q, y) + up + down
    crossed = pick(r, h) + send(pick(r, 1 - h), to_h)
    moved = send(crossed, to_own_row)

    moved, crossed, direct = together(moved, crossed, direct)
    row_summed = lax.all_gather(direct - moved, COL, axis=0, tiled=True)
    col_summed = gather_rows(send(direct, to_own_col) - crossed)
    over_p = (((0,), (0,)), ((), ()))
    near = given + lax.dot_general(row_factors, col_summed, over_p, precision=high)
    row_summed, near = together(row_summed, near)
    residual = near + lax.dot_general(row_summed, col_factors, over_p, precision=high)
    denominator = occ_energy[row] + occ_energy[col] - vir_energy[:, None] - vir_energy[None, :]
    return (residual / denominator)[None, None]


def solution(mesh):
    fine = Mesh(mesh.devices.reshape(SIZES), AXES)
    return jax.shard_map(
        shards,
        mesh=fine,
        in_specs=(P(ROW, COL), P(ROW, COL), P(COL, ROW), P(), P()),
        out_specs=P(ROW, COL),
        check_vma=False,
    )
```

```python
import jax
import jax.numpy as jnp
import numpy as np
from jax import lax
from jax.sharding import Mesh
from jax.sharding import PartitionSpec as P

AXES = ("y", "h", "k", "l", "x1", "x0")
SIZES = (4, 2, 2, 4, 2, 2)
ROW = ("y", "h", "k")
COL = ("l", "x1", "x0")


def send(value, to):
    pairs = []
    for source in range(256):
        y, h, k, l, x1, x0 = (int(v) for v in np.unravel_index(source, SIZES))
        y, h, k, l, x = to(y, h, k, l, 2 * x1 + x0)
        target = np.ravel_multi_index((y % 4, h % 2, k % 2, l % 4, (x % 4) >> 1, x % 2), SIZES)
        pairs.append((source, int(target)))
    return lax.ppermute(value, AXES, pairs)


def to_y(d):
    return lambda y, h, k, l, x: (y + d, h, k, l, x)


def to_x(d):
    return lambda y, h, k, l, x: (y, h, k, l, x + d)


def to_l(d):
    return lambda y, h, k, l, x: (y, h, k, l + d, x)


def to_h(y, h, k, l, x):
    return (y, h + 1, k, l, x)


def to_core(y, h, k, l, x):
    return (y, h, k + 1, l, x)


def pick(value, at):
    return lax.dynamic_index_in_dim(value, at, 0, keepdims=False)


def put(value, block, at):
    return lax.dynamic_update_index_in_dim(value, block, at, 0)


def place(y, h, k):
    return 8 * k + 4 * (y >> 1) + 2 * h + (y & 1)


def to_own_row(y, h, k, l, x):
    col = place(y, h, k)
    return (l, x >> 1, x & 1, col >> 2, col & 3)


def to_own_col(y, h, k, l, x):
    return (2 * (l & 1) + (x & 1), x >> 1, l >> 1, y, 2 * h + k)


def together(*values):
    return lax.optimization_barrier(values)


def get_y(q, y):
    _, n, _, b, columns = q.shape
    return lax.dynamic_slice(q, (y >> 1, 0, y & 1, 0, 0), (1, n, 1, b, columns)).reshape(n, b, columns)


def put_y(q, pair, y):
    n, b, columns = pair.shape
    return lax.dynamic_update_slice(q, pair.reshape(1, n, 1, b, columns), (y >> 1, 0, y & 1, 0, 0))


def shards(amplitudes, integrals, factors, occ_energy, vir_energy):
    high = lax.Precision.HIGH
    tile, given, block = amplitudes[0, 0], integrals[0, 0], factors[0]
    y, h, k, l, x1, x0 = (lax.axis_index(n) for n in AXES)
    row, col = 4 * y + 2 * h + k, 4 * l + 2 * x1 + x0
    b, columns = block.shape

    empty_half = jnp.zeros((2, 2, 2, b, columns), block.dtype)
    empty = jnp.zeros((2, 8 * b, columns), block.dtype)

    def gather_rows(block):
        other = send(block, to_h)
        pair = jnp.where(h == 0, jnp.stack([block, other]), jnp.stack([other, block]))
        f, g = together(send(pair, to_y(1)), send(pair, to_y(-1)))
        e = together(send(f[0], to_y(1)), send(g[1], to_y(-1)))
        q = empty_half
        for part, dy in ((pair, 0), (f, 3), (g, 1), (jnp.stack(e), 2)):
            q = put_y(q, part, (y + dy) % 4)
        q = q.reshape(8 * b, columns)
        return put(put(empty, q, k), send(q, to_core), 1 - k).reshape(16 * b, columns)

    def reduce_cols(part):
        x = 2 * x1 + x0
        q = part.reshape(4, 4, b, part.shape[1])

        def get_x(at):
            return lax.dynamic_index_in_dim(q, at % 4, 1, keepdims=False)

        far = get_x(x + 2)
        up, down = together(send(far[:2], to_x(1)), send(far[2:], to_x(-1)))
        after, before = get_x(x + 1), get_x(x + 3)
        after = jnp.concatenate([after[:2] + up, after[2:]])
        before = jnp.concatenate([before[:2], before[2:] + down])
        up, down = together(send(after, to_x(1)), send(before, to_x(-1)))
        r = get_x(x) + up + down
        return pick(r, l) + sum(together(*[send(pick(r, (l + d) % 4), to_l(d)) for d in range(1, 4)]))

    moved, tile, block = together(send(block, to_own_row), tile, block)
    row_factors = lax.all_gather(moved, COL, axis=0, tiled=True)
    col_factors = gather_rows(block)

    over_b, cut = (((1,), (1,)), ((), ())), 512 * columns // 768
    second = lax.dot_general(col_factors, 2.0 * tile[cut:], over_b, precision=high)
    first = lax.dot_general(col_factors, 2.0 * tile[:cut], over_b, precision=high)
    first = lax.psum_scatter(first, COL, scatter_dimension=0, tiled=True)
    second, row_factors = together(reduce_cols(second), row_factors)
    halves = row_factors.reshape(2, 8 * b, columns)
    over_a = (((1,), (0,)), ((), ()))
    theirs = lax.dot_general(pick(halves, 1 - k), tile, over_a, precision=high)
    theirs = send(theirs, to_core)
    q = lax.dot_general(pick(halves, k), tile, over_a, precision=high) + theirs
    q = q.reshape(2, 2, 2, b, columns)
    far = get_y(q, (y + 2) % 4)
    up, down = together(send(far[0], to_y(1)), send(far[1], to_y(-1)))
    after, before = get_y(q, (y + 1) % 4), get_y(q, (y + 3) % 4)
    after = jnp.stack([after[0] + up, after[1]])
    before = jnp.stack([before[0], before[1] + down])
    up, down = together(send(after, to_y(1)), send(before, to_y(-1)))
    r = get_y(q, y) + up + down
    crossed = pick(r, h) + send(pick(r, 1 - h), to_h)
    moved = send(crossed, to_own_row)

    direct = jnp.concatenate([first, second], axis=1)
    moved, crossed, direct = together(moved, crossed, direct)
    sent, whole = together(send(direct, to_own_col), direct - moved)
    row_summed = lax.all_gather(whole, COL, axis=0, tiled=True)
    col_summed = gather_rows(sent - crossed)
    over_p = (((0,), (0,)), ((), ()))
    near = given + lax.dot_general(row_factors, col_summed, over_p, precision=high)
    row_summed, near = together(row_summed, near)
    residual = near + lax.dot_general(row_summed, col_factors, over_p, precision=high)
    denominator = occ_energy[row] + occ_energy[col] - vir_energy[:, None] - vir_energy[None, :]
    return (residual / denominator)[None, None]


def solution(mesh):
    fine = Mesh(mesh.devices.reshape(SIZES), AXES)
    return jax.shard_map(
        shards,
        mesh=fine,
        in_specs=(P(ROW, COL), P(ROW, COL), P(COL, ROW), P(), P()),
        out_specs=P(ROW, COL),
        check_vma=False,
    )
```
